32 devices in a mesh: groups: 2 (over x), blk: 16 (over z, y, core).
Axes of the slice: x: 2, y: 2, z: 4, core: 2. Of those that a mesh axis runs over, the one named last changes fastest.
Arguments:
- queries: bfloat16 [32, 8192], P(('groups', 'blk')), parts along dimension 0, may hold values from -13 to 13
- cache_keys: bfloat16 [8192, 1024], P(('groups', 'blk')), parts along dimension 0, may hold values from -10 to 10
- cache_values: bfloat16 [8192, 1024], P(('groups', 'blk')), parts along dimension 0, may hold values from -5 to 5
- lengths: int32 [32], P(('groups', 'blk')), parts along dimension 0, may hold values from 1 to 256, as said below
- stretch_start: int32 [2], P('groups'), parts along dimension 0, may hold values from 2048 to 4080
- residual: float32 [32, 8192], P(('groups', 'blk')), parts along dimension 0, may hold values from -40 to 40
- out_weight: bfloat16 [8192, 8192], P('blk'), may hold values from -0.0625 to 0.0625
- norm_gain: float32 [8192], replicated, may hold values from 0.25 to 1.75
- gate_weight: bfloat16 [8192, 16384], P(None, 'blk'), may hold values from -0.0625 to 0.0625
- up_weight: bfloat16 [8192, 16384], P(None, 'blk'), may hold values from -0.0625 to 0.0625
- down_weight: bfloat16 [16384, 8192], P('blk'), may hold values from -0.046875 to 0.046875
Outputs:
- layer_out: float32 [32, 8192], P(('groups', 'blk')), parts along dimension 0
The draws below stay inside these ranges and needn't reach their ends.
There are 2 independent parts, one for each index of `groups`. The reference program is written for one: setup_inputs(seed, part) draws one part's arguments, and reference() takes and returns one part's arrays. A program takes and returns all parts, laid end to end along the dimension named above; an argument that names none is the same for every part. Nothing has to cross between parts.
Inputs may be any that keep to these rules, and one draw needn't show every extreme that they name: `lengths`: each shard holds 1 to 256 live slots, and some shard is full.
All inputs are finite; a program needn't handle non-finite values.
Results may differ from the reference program's by a relative error of at most 0.0025.
Values may be sent and summed in bfloat16 or wider, within the bound.
A program may use at most 128 MiB of HBM per device.

```python
import math
import jax
import jax.numpy as jnp
from jax import lax

MODEL_WIDTH = 8192
QUERY_HEADS = 64
KV_HEADS = 8
HEAD_DIM = 128
FFN_UNITS = 16384
CTX_DEV = 256
CONTEXT = 4096
STRETCH_ROWS = 16
SHARDS = 16


def draw_queries(key, part):
    sample = jax.random.truncated_normal(jax.random.fold_in(key, 11), -4.0, 4.0, (STRETCH_ROWS, QUERY_HEADS * HEAD_DIM), jnp.float32) * 3.0
    return sample.astype(jnp.bfloat16)


def draw_cache_keys(key, part):
    sample = jax.random.truncated_normal(jax.random.fold_in(key, 13), -4.0, 4.0, (CONTEXT, KV_HEADS * HEAD_DIM), jnp.float32)
    return sample.astype(jnp.bfloat16)


def draw_lengths(key, part):
    counts = jax.random.randint(jax.random.fold_in(key, 17), (SHARDS,), 1, CTX_DEV + 1)
    fullest = jax.random.randint(jax.random.fold_in(key, 19), (), 0, SHARDS)
    return jnp.where(jnp.arange(SHARDS) == fullest, CTX_DEV, counts).astype(jnp.int32)


def draw_residual(key, part):
    row_key = jax.random.fold_in(key, 23)
    col_key = jax.random.fold_in(key, 29)
    jitter_key = jax.random.fold_in(key, 31)
    col_scale = jnp.exp(jax.random.uniform(col_key, (1, MODEL_WIDTH), jnp.float32, math.log(0.3), math.log(3.0)))
    row_scale = jnp.exp(jax.random.uniform(row_key, (STRETCH_ROWS, 1), jnp.float32, math.log(0.3), math.log(3.0)))
    jitter = jax.random.truncated_normal(jitter_key, -4.0, 4.0, (STRETCH_ROWS, MODEL_WIDTH), jnp.float32)
    sample = jitter * col_scale * row_scale
    return sample.astype(jnp.float32)


def shard_levels(key, extent, shards, smallest, largest):
    factor_of = 1.0
    for axis_at, shards_of in shards:
        draws = jax.random.uniform(jax.random.fold_in(jax.random.fold_in(key, 6), axis_at), (shards_of,), jnp.float32, smallest / len(shards), largest / len(shards))
        factor_of = factor_of * jnp.repeat(jnp.exp(draws), extent[axis_at] // shards_of).reshape((-1,) + (1,) * (len(extent) - 1 - axis_at))
    return factor_of


def noise(stream_key, dims, width, bound, shards=(), held_as=jnp.bfloat16):
    values = jax.random.normal(stream_key, dims, jnp.float32) * width
    if len(shards) > 0:
        values = shard_levels(stream_key, dims, shards, -0.22, 0.18) * values
    return jnp.clip(values, min=-bound, max=bound).astype(held_as)


def setup_inputs(seed: int = 0, part: int = 0) -> dict:
    key_of = jax.random.split(jax.random.key(seed), 12)
    part_keys = jax.random.split(jax.random.fold_in(key_of[11], part), 12)
    queries = draw_queries(jax.random.fold_in(jax.random.fold_in(key_of[11], part), 71), part)
    cache_keys = draw_cache_keys(jax.random.fold_in(jax.random.fold_in(key_of[11], part), 71), part)
    cache_values = noise(part_keys[2], (CONTEXT, KV_HEADS * HEAD_DIM), 1.0, 5.0, ((0, 16),))
    lengths = draw_lengths(jax.random.fold_in(jax.random.fold_in(key_of[11], part), 71), part)
    stretch_start = jax.random.randint(part_keys[4], (1,), CONTEXT // 2, CONTEXT - STRETCH_ROWS + 1).astype(jnp.int32)
    residual = draw_residual(jax.random.fold_in(jax.random.fold_in(key_of[11], part), 71), part)
    out_weight = noise(key_of[6], (QUERY_HEADS * HEAD_DIM, MODEL_WIDTH), (QUERY_HEADS * HEAD_DIM) ** -0.5, 0.0625, ((0, 16),))
    norm_gain = jnp.clip(1.0 + 0.15 * jax.random.normal(key_of[7], (MODEL_WIDTH,), jnp.float32), 0.25, 1.75)
    gate_weight = noise(key_of[8], (MODEL_WIDTH, FFN_UNITS), MODEL_WIDTH ** -0.5, 0.0625, ((1, 16),))
    up_weight = noise(key_of[9], (MODEL_WIDTH, FFN_UNITS), MODEL_WIDTH ** -0.5, 0.0625, ((1, 16),))
    down_weight = noise(key_of[10], (FFN_UNITS, MODEL_WIDTH), FFN_UNITS ** -0.5, 0.046875, ((0, 16),))
    return {"queries": queries, "cache_keys": cache_keys, "cache_values": cache_values, "lengths": lengths, "stretch_start": stretch_start, "residual": residual, "out_weight": out_weight, "norm_gain": norm_gain, "gate_weight": gate_weight, "up_weight": up_weight, "down_weight": down_weight}


NEG_FLOOR = -1e+30
EPSILON = 1e-05

def reference(queries, cache_keys, cache_values, lengths, stretch_start, residual, out_weight, norm_gain, gate_weight, up_weight, down_weight):
    group_size = QUERY_HEADS // KV_HEADS
    score_scale = 1.0 / math.sqrt(HEAD_DIM)
    row_count = queries.shape[0]
    query_heads = queries.astype(jnp.float32).reshape(row_count, KV_HEADS, group_size, HEAD_DIM)
    key_blocks = cache_keys.reshape(SHARDS, CTX_DEV, KV_HEADS, HEAD_DIM)
    value_blocks = cache_values.reshape(SHARDS, CTX_DEV, KV_HEADS, HEAD_DIM)
    row_position = stretch_start[0] + jnp.arange(row_count, dtype=jnp.int32)
    slot_index = jnp.arange(CTX_DEV, dtype=jnp.int32)
    shard_ids = jnp.arange(SHARDS, dtype=jnp.int32)

    def visit(state_in, block_in):
        running_max, numer_acc, denom_acc = state_in
        key_blk, value_blk, live_count, shard_id = block_in
        scores = jnp.einsum('rhgd,khd->rhgk', query_heads, key_blk.astype(jnp.float32)) * score_scale
        position = shard_id * CTX_DEV + slot_index
        visible = (slot_index[None, :] < live_count) & (position[None, :] <= row_position[:, None])
        masked = visible[:, None, None, :]
        local_max = lax.optimization_barrier(jnp.max(jnp.where(masked, scores, NEG_FLOOR), axis=-1))
        weights = jnp.where(masked, jnp.exp(scores - local_max[..., None]), 0.0).astype(jnp.bfloat16)
        weights = lax.optimization_barrier(weights).astype(jnp.float32)
        part_num = jnp.einsum('rhgk,khd->rhgd', weights, value_blk.astype(jnp.float32))
        part_den = lax.optimization_barrier(jnp.sum(weights, axis=-1))
        new_max = jnp.maximum(running_max, local_max)
        old_factor = jnp.exp(running_max - new_max)
        new_factor = jnp.exp(local_max - new_max)
        numer_acc = numer_acc * old_factor[..., None] + part_num * new_factor[..., None]
        denom_acc = denom_acc * old_factor + part_den * new_factor
        return ((new_max, numer_acc, denom_acc), None)
    start_state = (jnp.full((row_count, KV_HEADS, group_size), NEG_FLOOR, jnp.float32), jnp.zeros((row_count, KV_HEADS, group_size, HEAD_DIM), jnp.float32), jnp.zeros((row_count, KV_HEADS, group_size), jnp.float32))
    final_state, _ = lax.scan(visit, start_state, (key_blocks, value_blocks, lengths, shard_ids))
    numerator = final_state[1]
    denominator = final_state[2]
    attention = (numerator / denominator[..., None]).reshape(row_count, QUERY_HEADS * HEAD_DIM).astype(jnp.bfloat16)
    projected = jnp.dot(attention, out_weight, preferred_element_type=jnp.float32)
    mixed = residual + projected
    normed = (mixed * lax.rsqrt(lax.optimization_barrier(jnp.mean(mixed * mixed, axis=-1, keepdims=True)) + EPSILON) * norm_gain).astype(jnp.bfloat16)
    gate_term = jnp.dot(normed, gate_weight, preferred_element_type=jnp.float32)
    up_term = jnp.dot(normed, up_weight, preferred_element_type=jnp.float32)
    activation = (jax.nn.silu(gate_term) * up_term).astype(jnp.bfloat16)
    return mixed + jnp.dot(activation, down_weight, preferred_element_type=jnp.float32)
```

```python
import functools

import jax
import jax.numpy as jnp
from jax import lax
from jax.experimental import pallas as pl
from jax.experimental.pallas import tpu as pltpu
from jax.sharding import PartitionSpec as P

QUERY_HEADS = 64
KV_HEADS = 8
HEAD_DIM = 128
GROUP = QUERY_HEADS // KV_HEADS
WIDTH = QUERY_HEADS * HEAD_DIM
NEG_FLOOR = -1e30
EPSILON = 1e-05
F32 = jnp.float32
BF16 = jnp.bfloat16
MESH = pl.DeviceIdType.MESH


def kernel(
    n, ctx, cols, hpd, chunk,
    len_ref, start_ref, q_ref, res_ref, gain_ref, k_hbm, v_hbm, wo_hbm, wg_hbm, wu_hbm, wd_hbm,
    out_ref,
    k_buf, v_buf, wo_buf, wg_buf, wu_buf, wd_buf,
    q_recv, row_f32, qh, msg, msg_recv, part, proj_recv, norm_row, norm_recv, x_buf, ffn_part,
    ffn_recv, hid_buf,
    load_sem, send_sem, recv_sem,
):
    me = lax.axis_index("blk")
    half = wo_buf.shape[0]

    k_load = pltpu.make_async_copy(k_hbm, k_buf, load_sem.at[0])
    v_load = pltpu.make_async_copy(v_hbm, v_buf, load_sem.at[1])
    wo_load = pltpu.make_async_copy(wo_hbm, wo_buf, load_sem.at[2])
    wg_load = pltpu.make_async_copy(wg_hbm, wg_buf, load_sem.at[3])
    wu_load = pltpu.make_async_copy(wu_hbm, wu_buf, load_sem.at[4])
    wd_load = pltpu.make_async_copy(wd_hbm.at[pl.ds(0, half)], wd_buf, load_sem.at[5])
    wd2_load = pltpu.make_async_copy(wd_hbm.at[pl.ds(half, half)], wo_buf, load_sem.at[6])
    for load in (k_load, v_load, wo_load, wg_load, wu_load, wd_load):
        load.start()

    barrier = pltpu.get_barrier_semaphore()

    def greet(i, c):
        pl.semaphore_signal(
            barrier, inc=1, device_id={"blk": lax.rem(me + i, n)}, device_id_type=MESH
        )
        return c

    lax.fori_loop(1, n, greet, 0)
    pl.semaphore_wait(barrier, n - 1)

    def send(phase, src, dst, to):
        pltpu.make_async_remote_copy(
            src_ref=src,
            dst_ref=dst,
            send_sem=send_sem.at[phase],
            recv_sem=recv_sem.at[phase],
            device_id={"blk": to},
            device_id_type=MESH,
        ).start()

    def await_all(sem, buf):
        view = buf.at[pl.ds(0, n - 1)]
        pltpu.make_async_copy(view, view, sem).wait()

    def send_to_all(phase, src, buf):
        def step(i, c):
            send(phase, src, buf.at[me], lax.rem(me + i, n))
            return c

        lax.fori_loop(1, n, step, 0)

    def scatter(phase, parts, buf):
        def step(i, c):
            to = lax.rem(me + i, n)
            send(phase, parts.at[to], buf.at[me], to)
            return c

        lax.fori_loop(1, n, step, 0)

    send_to_all(0, q_ref, q_recv)
    q_recv[me] = q_ref[...]
    await_all(recv_sem.at[0], q_recv)
    row_f32[...] = q_recv[...].astype(F32)
    for h in range(QUERY_HEADS):
        g, i = divmod(h, GROUP)
        qh[g, i * n : (i + 1) * n, :] = row_f32[:, h, :].astype(BF16)
    k_load.wait()
    v_load.wait()

    slot = lax.broadcasted_iota(jnp.int32, (GROUP * n, ctx), 1)
    row = lax.rem(lax.broadcasted_iota(jnp.int32, (GROUP * n, ctx), 0), n)
    visible = (slot < len_ref[0]) & (me * ctx + slot <= start_ref[0] + row)
    lane = lax.broadcasted_iota(jnp.int32, (n, HEAD_DIM), 1)
    dpg = n // KV_HEADS
    per_head = max(HEAD_DIM // cols, 1)

    def head_step(step, carry):
        g = lax.rem(me // dpg + 1 + step, KV_HEADS)
        at = pl.ds(pl.multiple_of(g * HEAD_DIM, HEAD_DIM), HEAD_DIM)
        scores = lax.dot_general(
            qh[g], k_buf[:, at], (((1,), (1,)), ((), ())), preferred_element_type=F32
        ) * (HEAD_DIM ** -0.5)
        peak = jnp.max(jnp.where(visible, scores, NEG_FLOOR), axis=1, keepdims=True)
        peak = peak.astype(BF16).astype(F32)
        weights = jnp.where(visible, jnp.exp(scores - peak), 0.0).astype(BF16)
        total = jnp.sum(weights.astype(F32), axis=1, keepdims=True)
        numer = jnp.dot(weights, v_buf[:, at], preferred_element_type=F32)
        total_hi = total.astype(BF16).astype(F32)
        total_lo = total - total_hi
        for d in range(dpg):
            to = g * dpg + d
            stats = jnp.zeros((n, HEAD_DIM), F32)
            for i in range(hpd):
                h = d * hpd + i if per_head == 1 else d // per_head
                rows = slice(h * n, (h + 1) * n)
                block = numer[rows, :]
                if per_head > 1:
                    lo = (d % per_head) * cols
                    block = block[:, lo : lo + cols]
                msg[to, :, HEAD_DIM * (i + 1) : HEAD_DIM * (i + 1) + block.shape[1]] = block.astype(BF16)
                stats = jnp.where(lane == i, peak[rows, :], stats)
                stats = jnp.where(lane == hpd + i, total_hi[rows, :], stats)
                stats = jnp.where(lane == 2 * hpd + i, total_lo[rows, :], stats)
            msg[to, :, 0:HEAD_DIM] = stats.astype(BF16)

            @pl.when(to != me)
            def _():
                send(1, msg.at[to], msg_recv.at[me], to)

        return carry

    lax.fori_loop(0, KV_HEADS, head_step, 0)
    msg_recv[me] = msg[me]
    await_all(recv_sem.at[1], msg_recv)

    def top_step(d, top):
        return jnp.maximum(top, msg_recv[d, :, 0:HEAD_DIM].astype(F32))

    top = lax.fori_loop(0, n, top_step, jnp.full((n, HEAD_DIM), NEG_FLOOR, F32))
    piece = min(cols, HEAD_DIM)

    def join_step(d, state):
        stats = msg_recv[d, :, 0:HEAD_DIM].astype(F32)
        factor = jnp.exp(jnp.minimum(stats - top, 0.0))
        joined = []
        for i in range(hpd):
            f = factor[:, i : i + 1]
            den = stats[:, hpd + i : hpd + i + 1] + stats[:, 2 * hpd + i : 2 * hpd + i + 1]
            num = msg_recv[d, :, HEAD_DIM * (i + 1) : HEAD_DIM * (i + 1) + piece].astype(F32)
            joined += [state[2 * i] + f * num, state[2 * i + 1] + f * den]
        return tuple(joined)

    zero = (jnp.zeros((n, piece), F32), jnp.zeros((n, 1), F32)) * hpd
    state = lax.fori_loop(0, n, join_step, zero)
    attn = jnp.concatenate(
        [(state[2 * i] / state[2 * i + 1]).astype(BF16) for i in range(hpd)], axis=1
    )

    wo_load.wait()
    for c in range(WIDTH // chunk):
        p = jnp.dot(attn, wo_buf[:, c * chunk : (c + 1) * chunk], preferred_element_type=F32)
        for s in range(chunk // HEAD_DIM):
            row_f32[:, c * (chunk // HEAD_DIM) + s, :] = p[:, s * HEAD_DIM : (s + 1) * HEAD_DIM]
    wd2_load.start()
    part[...] = row_f32[...].astype(BF16)
    scatter(2, part, proj_recv)
    proj_recv[me] = part[me]
    await_all(recv_sem.at[2], proj_recv)

    def add_rows(buf, base):
        def step(d, acc):
            return acc + buf[d].astype(F32)

        return lax.fori_loop(0, n, step, base)

    mixed = res_ref[...] + add_rows(proj_recv, jnp.zeros((QUERY_HEADS, HEAD_DIM), F32))
    mean = jnp.sum(
        jnp.sum(mixed * mixed, axis=1, keepdims=True), axis=0, keepdims=True
    ) * (1.0 / WIDTH)
    norm_row[...] = (mixed * lax.rsqrt(mean + EPSILON) * gain_ref[...]).astype(BF16)
    send_to_all(3, norm_row, norm_recv)
    norm_recv[me] = norm_row[...]
    out_ref[...] = mixed
    await_all(recv_sem.at[3], norm_recv)
    row_f32[...] = norm_recv[...].astype(F32)
    for h in range(QUERY_HEADS):
        x_buf[:, h * HEAD_DIM : (h + 1) * HEAD_DIM] = row_f32[:, h, :].astype(BF16)

    wg_load.wait()
    wu_load.wait()
    hidden = wg_buf.shape[1]
    tile = min(hidden, 256)

    def hidden_step(j, c):
        at = pl.ds(pl.multiple_of(j * tile, tile), tile)
        gate = jnp.dot(x_buf[...], wg_buf[:, at], preferred_element_type=F32)
        up = jnp.dot(x_buf[...], wu_buf[:, at], preferred_element_type=F32)
        hid_buf[:, at] = (gate / (1.0 + jnp.exp(-gate)) * up).astype(BF16)
        return c

    lax.fori_loop(0, hidden // tile, hidden_step, 0)
    wd_load.wait()
    wd2_load.wait()
    act = hid_buf[...]
    for c in range(WIDTH // chunk):
        at = slice(c * chunk, (c + 1) * chunk)
        p = jnp.dot(act[:, :half], wd_buf[:, at], preferred_element_type=F32) + jnp.dot(
            act[:, half:], wo_buf[:, at], preferred_element_type=F32
        )
        for s in range(chunk // HEAD_DIM):
            row_f32[:, c * (chunk // HEAD_DIM) + s, :] = p[:, s * HEAD_DIM : (s + 1) * HEAD_DIM]
    ffn_part[...] = row_f32[...].astype(BF16)
    scatter(4, ffn_part, ffn_recv)
    ffn_recv[me] = ffn_part[me]
    await_all(recv_sem.at[4], ffn_recv)
    out_ref[...] = out_ref[...] + add_rows(ffn_recv, jnp.zeros((QUERY_HEADS, HEAD_DIM), F32))
    for phase, buf in enumerate((q_recv, msg_recv, proj_recv, norm_recv, ffn_recv)):
        await_all(send_sem.at[phase], buf)


def body(
    n, queries, cache_keys, cache_values, lengths, stretch_start, residual, out_weight, norm_gain,
    gate_weight, up_weight, down_weight,
):
    ctx = cache_keys.shape[0]
    cols = WIDTH // n
    hpd = max(cols // HEAD_DIM, 1)
    chunk = 1024
    block = (QUERY_HEADS, HEAD_DIM)
    vmem = pl.BlockSpec(memory_space=pltpu.VMEM)
    smem = pl.BlockSpec(memory_space=pltpu.SMEM)
    any_ = pl.BlockSpec(memory_space=pl.ANY)
    hidden = gate_weight.shape[1]
    half = out_weight.shape[0]
    rows_of = pltpu.VMEM((n, *block), BF16)
    out = pl.pallas_call(
        functools.partial(kernel, n, ctx, cols, hpd, chunk),
        out_shape=jax.ShapeDtypeStruct(block, F32),
        in_specs=[smem, smem, vmem, vmem, vmem] + [any_] * 6,
        out_specs=vmem,
        scratch_shapes=[
            pltpu.VMEM(cache_keys.shape, BF16),
            pltpu.VMEM(cache_values.shape, BF16),
            pltpu.VMEM(out_weight.shape, BF16),
            pltpu.VMEM(gate_weight.shape, BF16),
            pltpu.VMEM(up_weight.shape, BF16),
            pltpu.VMEM((half, WIDTH), BF16),
            rows_of,
            pltpu.VMEM((n, *block), F32),
            pltpu.VMEM((KV_HEADS, GROUP * n, HEAD_DIM), BF16),
            pltpu.VMEM((n, n, HEAD_DIM * (hpd + 1)), BF16),
            pltpu.VMEM((n, n, HEAD_DIM * (hpd + 1)), BF16),
            rows_of,
            rows_of,
            pltpu.VMEM(block, BF16),
            rows_of,
            pltpu.VMEM((n, WIDTH), BF16),
            rows_of,
            rows_of,
            pltpu.VMEM((n, hidden), BF16),
            pltpu.SemaphoreType.DMA((7,)),
            pltpu.SemaphoreType.DMA((5,)),
            pltpu.SemaphoreType.DMA((5,)),
        ],
        compiler_params=pltpu.CompilerParams(
            collective_id=0, has_side_effects=True, vmem_limit_bytes=60 * 1024 * 1024
        ),
    )(
        lengths, stretch_start, queries.reshape(block), residual.reshape(block),
        norm_gain.reshape(block), cache_keys, cache_values, out_weight, gate_weight, up_weight,
        down_weight,
    )
    return out.reshape(1, WIDTH)


def solution(mesh):
    in_specs = (
        P(("groups", "blk"), None),
        P(("groups", "blk"), None),
        P(("groups", "blk"), None),
        P(("groups", "blk")),
        P("groups"),
        P(("groups", "blk"), None),
        P("blk", None),
        P(),
        P(None, "blk"),
        P(None, "blk"),
        P("blk", None),
    )
    out_specs = P(("groups", "blk"), None)
    return jax.shard_map(
        functools.partial(body, mesh.shape["blk"]),
        mesh=mesh,
        in_specs=in_specs,
        out_specs=out_specs,
        check_vma=False,
    )
```
